1024 devices in a mesh: blk: 32 (over x_lo, z), rep: 32 (over x_hi, y, core).
Axes of the slice: x: 4 (x_hi: 2, x_lo: 2; x = x_hi * 2 + x_lo), y: 8, z: 16, core: 2. Of those that a mesh axis runs over, the one named last changes fastest.
Arguments:
- amps: bfloat16 [1024, 65536], P(None, ('rep', 'blk')), may hold values from -6 to 6
- amp_tiles: int32 [1024, 1024], P(None, ('rep', 'blk')), may hold values 0 or 1
- ints: bfloat16 [65536, 16384], P('rep', 'blk'), may hold values from -0.0234375 to 0.0234375
- int_tiles: int32 [1024, 256], P('rep', 'blk'), may hold values from 0 to 1, as said below
Outputs:
- ladder: float32 [1024, 16384], P('rep', 'blk')
The draws below stay inside these ranges and needn't reach their ends.
Inputs may be any that keep to these rules, and one draw needn't show every extreme that they name: `int_tiles`: each entry is 0 or 1; the share of kept tiles differs from one residual column tile to another.
All inputs are finite; a program needn't handle non-finite values. No bound on the sum of `amp_tiles` on one device may be relied on, other than what follows from the above.
Results may differ from the reference program's by a relative error of at most 0.0003.
Values may be sent and summed in bfloat16 or wider, within the bound.
No kernel may reach another device: no remote copies, remote signals or barrier semaphores. Data moves between devices by JAX's collectives and lax.ppermute only.
A program may use at most 32 MiB of HBM per device.

```python
import jax
import jax.numpy as jnp
from jax import lax

TILE = 64
AB_DEV = 8
P_SIZE = 1024
NCD_T = 1024
NAB_T = 256


def draw_int_tiles(key, part):
    key = jax.random.fold_in(key, 7)
    level_key, flag_key = jax.random.split(key)
    levels = jax.random.randint(level_key, (1, NAB_T), 1, 6)
    rolls = jax.random.randint(flag_key, (NCD_T, NAB_T), 0, 6)
    return (rolls < levels).astype(jnp.int32)


def touch_ends(result, rng, least, high):
    shape = result.shape
    spot = [jax.random.randint(jax.random.fold_in(rng, axis), (), 0, shape[axis]) for axis in range(len(shape))]
    result = result.at[tuple(spot)].set(least)
    longest = shape.index(max(shape))
    spot[longest] = (spot[longest] + 1) % shape[longest]
    return result.at[tuple(spot)].set(high)


def block_scale(rng, dims, pieces, least, top_value):
    def one(axis_at, parts):
        heights = jax.random.uniform(jax.random.fold_in(jax.random.fold_in(rng, 6), axis_at), (parts,), jnp.float32, least / len(pieces), top_value / len(pieces))
        return jnp.repeat(jnp.exp(heights), dims[axis_at] // parts).reshape((-1,) + (1,) * (len(dims) - axis_at - 1))

    factor_of = one(*pieces[0])
    for cut in pieces[1:]:
        factor_of = factor_of * one(*cut)
    return factor_of


def scatter_about(own_key, dims, width, limit, shards=(), kind=jnp.bfloat16):
    gain = block_scale(own_key, dims, shards, -0.22, 0.18) if shards else 1.0
    drawn = jax.random.normal(own_key, dims, jnp.float32) * width * gain
    return jnp.minimum(jnp.maximum(drawn, -limit), limit).astype(kind)


def setup_inputs(seed: int = 0) -> dict:
    seeds = jax.random.split(jax.random.key(seed), 5)
    return {
        "amps": scatter_about(seeds[0], (P_SIZE, NCD_T * TILE), 1.0, 6.0, ((1, 1024),)),
        "amp_tiles": touch_ends((jax.random.randint(seeds[1], (P_SIZE, NCD_T), 0, 4) < 3).astype(jnp.int32), jax.random.fold_in(seeds[1], 1), 0, 1),
        "ints": scatter_about(seeds[2], (NCD_T * TILE, NAB_T * TILE), (NCD_T * TILE) ** -0.5, 0.0234375, ((0, 32), (1, 32))),
        "int_tiles": draw_int_tiles(jax.random.fold_in(seeds[4], 71), 0),
    }


def reference(amps, amp_tiles, ints, int_tiles):
    amp_mask = jnp.repeat(amp_tiles, TILE, axis=1)
    amp_full = jnp.where(amp_mask > 0, amps, jnp.zeros_like(amps)).astype(jnp.float32)
    block_width = AB_DEV * TILE
    block_count = NAB_T // AB_DEV

    def one_block(block_index):
        offset = (block_index * block_width).astype(jnp.int32)
        columns = lax.dynamic_slice_in_dim(ints, offset, block_width, 1)
        tile_flags = lax.dynamic_slice_in_dim(int_tiles, (block_index * AB_DEV).astype(jnp.int32), AB_DEV, 1)
        column_mask = jnp.repeat(jnp.repeat(tile_flags, TILE, axis=0), TILE, axis=1)
        columns = jnp.where(column_mask > 0, columns, jnp.zeros_like(columns)).astype(jnp.float32)
        return jnp.dot(amp_full, columns, precision=lax.Precision.HIGHEST)

    column_blocks = lax.map(one_block, jnp.arange(block_count, dtype=jnp.int32))
    return jnp.transpose(column_blocks, (1, 0, 2)).reshape(P_SIZE, block_count * block_width)
```

```python
import jax
import jax.numpy as jnp
from jax import lax
from jax.sharding import PartitionSpec as P

TILE = 64
Z = 16
SHIFT = 13
SPAN = 29
LEAST = -26
ZERO_MARK = 65504.0


def power_below(t):
    power = jnp.full_like(t, 2.0**-13)
    for step in (16, 8, 4, 2, 1):
        higher = power * 2.0**step
        power = jnp.where(t >= higher, higher, power)
    return power


def encode(x):
    value = x.astype(jnp.float32)
    size = jnp.abs(value)
    level = jnp.zeros(x.shape, jnp.int32)
    for j in range(4):
        level += ((size < 2.0 ** (LEAST - SPAN * j)) & (size > 0)).astype(jnp.int32)
    rare = jnp.any(level > 0)
    raised = value
    for j in range(1, 5):
        raised = jnp.where(level == j, value * 2.0 ** (SPAN * j), raised)
    raised = raised * 2.0**SHIFT
    low = jnp.where(level == 4, -1, level)
    first = (lax.broadcasted_iota(jnp.int32, x.shape, 0) + lax.broadcasted_iota(jnp.int32, x.shape, 1)) == 0
    marked = first & rare
    low = jnp.where(marked & (level == 0), -2, low)
    bits = low.astype(jnp.float32) * power_below(jnp.abs(raised)) * 2.0**-10
    code = jnp.where(raised < 0, raised - bits, raised + bits)
    code = jnp.where(size > 0, code, jnp.where(marked, ZERO_MARK, 0.0))
    return code.astype(jnp.float16)


def decode_rare(code):
    h = code.astype(jnp.float32)
    t = h.astype(jnp.bfloat16).astype(jnp.float32)
    low = (jnp.abs(h) - jnp.abs(t)) * 2.0**10 / power_below(jnp.abs(t))
    value = t
    for level, bits in ((1, 1.0), (2, 2.0), (3, 3.0), (4, -1.0)):
        value = jnp.where(low == bits, t * 2.0 ** (-SPAN * level), value)
    value = jnp.where(h == ZERO_MARK, 0.0, value)
    return value.astype(jnp.bfloat16)


def per_device(amps, amp_tiles, ints, int_tiles):
    x_lo = lax.axis_index("blk") // Z
    core = lax.axis_index("rep") % 2
    rows = amps.shape[0]
    cols = ints.shape[1]

    own = encode(jnp.where(amp_tiles.T > 0, amps.T, jnp.zeros_like(amps.T)))
    other = lax.ppermute(own, "blk", [(b, b ^ Z) for b in range(2 * Z)])
    pair = jnp.where(x_lo == 0, jnp.concatenate([own, other]), jnp.concatenate([other, own]))
    rings = [[h * Z + z for z in range(Z)] for h in range(2)]
    codes = lax.all_gather(pair[None], "blk", axis=0, tiled=True, axis_index_groups=rings)

    flags = jnp.repeat((int_tiles > 0).reshape(2, Z, -1), TILE, axis=2)
    blocks = ints.reshape(2, Z, TILE, cols)
    kept = jnp.where(flags[:, :, None, :], blocks, jnp.zeros_like(blocks))
    kept = kept.transpose(1, 0, 2, 3).reshape(-1, cols)
    kept = lax.optimization_barrier(kept)

    heads = codes.reshape(2 * Z, TILE, rows)[:, 0, :1].astype(jnp.float32)
    rare = jnp.any(heads != heads.astype(jnp.bfloat16).astype(jnp.float32))

    def product(table):
        return lax.dot_general(
            table.reshape(-1, rows), kept, (((0,), (0,)), ((), ())), preferred_element_type=jnp.float32
        )

    total = lax.cond(
        rare,
        lambda c: product(decode_rare(c)),
        lambda c: product(c.astype(jnp.bfloat16)),
        codes,
    )

    parts = total.reshape(16, 2, -1, cols)
    mine = lax.dynamic_index_in_dim(parts, core, 1, keepdims=False)
    theirs = lax.dynamic_index_in_dim(parts, 1 - core, 1, keepdims=False)
    mine = mine + lax.ppermute(theirs, "rep", [(r, r ^ 1) for r in range(32)])
    peers = [[c + 2 * i for i in range(16)] for c in range(2)]
    shares = lax.all_to_all(mine, "rep", 0, 0, tiled=True, axis_index_groups=peers)
    return jnp.sum(shares, axis=0) * 2.0**-SHIFT


def solution(mesh):
    return jax.shard_map(
        per_device,
        mesh=mesh,
        in_specs=(
            P(None, ("rep", "blk")),
            P(None, ("rep", "blk")),
            P("rep", "blk"),
            P("rep", "blk"),
        ),
        out_specs=P("rep", "blk"),
        check_vma=False,
    )
```

```python
import jax
import jax.numpy as jnp
from jax import lax
from jax.experimental import pallas as pl
from jax.experimental.pallas import tpu as pltpu
from jax.sharding import PartitionSpec as P

TILE = 64
Z = 16
CHIPS = 16
Y = 8
PEERS = 32
ROWS = 32
LANES = 128
BIAS = 253.0
STEP = 512
VMEM = 40 * 1024 * 1024
WHOLE = 62 * 1024 * 1024


def encode(amps, tiles):
    value = jnp.where(tiles > 0, amps.astype(jnp.float32), 0.0)
    size = jnp.maximum(jnp.abs(value), 2.0**-126)
    power = jnp.floor(jnp.log2(size))
    half = jnp.floor(power * 0.5)
    digits = jnp.round(size * jnp.exp2(-half) * jnp.exp2(half - power) * 128.0)
    high = digits >= 256.0
    low = digits < 128.0
    digits = jnp.where(high, digits * 0.5, jnp.where(low, digits * 2.0, digits))
    power = jnp.where(high, power + 1.0, jnp.where(low, power - 1.0, power))
    code = (power + (BIAS - 1.0)) * 128.0 + digits
    code = jnp.where(value < 0, -code, code)
    code = jnp.where(jnp.abs(value) < 2.0**-126, 0.0, code)
    return code.astype(jnp.int32).astype(jnp.int16)


def decode(codes):
    number = codes.astype(jnp.float32) * (1.0 / 128.0)
    whole = jnp.floor(jnp.abs(number))
    digits = number + jnp.where(number < 0, whole - 1.0, 1.0 - whole)
    return (digits * jnp.exp2(whole - BIAS)).astype(jnp.bfloat16)


def spread(tiles):
    shape = (tiles.shape[0], tiles.shape[0] * TILE)
    at = lax.broadcasted_iota(jnp.int32, shape, 1) // TILE == lax.broadcasted_iota(jnp.int32, shape, 0)
    return lax.dot_general(
        tiles.astype(jnp.float32), at.astype(jnp.float32), (((0,), (0,)), ((), ())), preferred_element_type=jnp.float32
    )


def keep(block, flags):
    rows = []
    for t in range(block.shape[0] // TILE):
        part = block[t * TILE : (t + 1) * TILE, :].astype(jnp.float32)
        rows.append(jnp.where(flags[t : t + 1, :] > 0, part, 0.0).astype(jnp.bfloat16))
    return jnp.concatenate(rows, axis=0)


def front_body(place, amps, tiles, ints, flags, codes, away, wide):
    step = pl.program_id(0)

    @pl.when(step == 0)
    def _():
        wide[...] = spread(flags[...])

    count = ints.shape[0] // TILE
    first = pl.multiple_of((1 - place[0] // 2) * Z + step * count, 8)
    away[...] = keep(ints[...], wide[pl.ds(first, count), :])
    codes[...] = encode(amps[...], tiles[...])


def product_body(place, codes, ints, flags, swapped, mine, theirs, kept, wide):
    x_lo = place[0] // 2
    core = place[0] % 2

    @pl.when(pl.program_id(0) == 0)
    def _():
        wide[...] = spread(flags[...])
        kept[...] = keep(ints[...], wide[pl.ds(pl.multiple_of(x_lo * Z, 8), Z), :])

    amps = decode(codes[...])

    def put(side, block):
        total = lax.dot_general(amps, block, (((0,), (0,)), ((), ())), preferred_element_type=jnp.float32)
        total = total.reshape(STEP // (2 * ROWS), 2, ROWS, total.shape[-1])
        mine[side] = jnp.where(core == 0, total[:, 0], total[:, 1])
        theirs[side] = jnp.where(core == 0, total[:, 1], total[:, 0])

    put(x_lo, kept[...])
    put(1 - x_lo, swapped[...])


def diagonal():
    shape = (ROWS, LANES)
    return lax.broadcasted_iota(jnp.int32, shape, 0) == lax.broadcasted_iota(jnp.int32, shape, 1)


def pack(totals, shares):
    lines = []
    at = 0
    for total in totals:
        top = jnp.max(jnp.abs(total), axis=1, keepdims=True)
        level = jnp.ceil(jnp.log2(jnp.maximum(top, 2.0**-110)) * 16.0)
        scaled = total * jnp.exp2(-level * (1.0 / 16.0)) * 32767.0
        whole = jnp.clip(jnp.round(scaled), -32767.0, 32767.0).astype(jnp.int32).astype(jnp.int16)
        for k in range(total.shape[1] // LANES):
            shares[at : at + ROWS, :] = whole[:, LANES * k : LANES * (k + 1)]
            at += ROWS
        lines.append(jnp.sum(jnp.where(diagonal(), level, 0.0), axis=0, keepdims=True))
    lines.append(jnp.zeros((16 - len(lines), LANES), jnp.float32))
    shares[at:, :] = jnp.concatenate(lines, axis=0).astype(jnp.int32).astype(jnp.int16)


def unpack(shares, i, parts):
    at = shares.shape[0] - 16
    line = shares[at:, :].astype(jnp.float32)[i : i + 1, :]
    level = jnp.sum(jnp.where(diagonal(), line, 0.0), axis=1, keepdims=True)
    scale = jnp.exp2(level * (1.0 / 16.0)) * (1.0 / 32767.0)
    at = i * parts * ROWS
    rows = [shares[at + ROWS * k : at + ROWS * (k + 1), :].astype(jnp.float32) * scale for k in range(parts)]
    return jnp.concatenate(rows, axis=1)


def pack_body(mine, theirs, shares):
    pack([mine[0, i] + theirs[0, i] for i in range(mine.shape[1])], shares.at[0])


def middle_body(came, shares):
    parts = (shares.shape[1] - 16) // ROWS
    for i in range(shares.shape[0]):
        total = sum(unpack(came.at[j], i, parts) for j in range(came.shape[0]))
        pack([total], shares.at[i])


def last_body(shares, out):
    out[...] = sum(unpack(shares.at[i], 0, out.shape[1] // LANES) for i in range(shares.shape[0]))


def per_device(amps, amp_tiles, ints, int_tiles):
    blk = lax.axis_index("blk")
    rep = lax.axis_index("rep")
    x_lo = lax.shift_right_logical(blk, 4)
    core = rep & 1
    place = (2 * x_lo + core).astype(jnp.int32).reshape(1)
    pairs = amps.shape[0]
    cols = ints.shape[1]
    half = ints.shape[0] // 2
    parts = cols // LANES
    tile_flags = int_tiles.T

    codes, away = pl.pallas_call(
        front_body,
        grid_spec=pltpu.PrefetchScalarGridSpec(
            num_scalar_prefetch=1,
            grid=(2,),
            in_specs=[
                pl.BlockSpec((TILE // 2, pairs), lambda s, place: (s, 0)),
                pl.BlockSpec((1, pairs), lambda s, place: (0, 0)),
                pl.BlockSpec((half // 2, cols), lambda s, place: (2 * (1 - place[0] // 2) + s, 0)),
                pl.BlockSpec(tile_flags.shape, lambda s, place: (0, 0)),
            ],
            out_specs=[
                pl.BlockSpec((TILE // 2, pairs), lambda s, place: (s, 0)),
                pl.BlockSpec((half // 2, cols), lambda s, place: (s, 0)),
            ],
            scratch_shapes=[pltpu.VMEM((2 * Z, cols), jnp.float32)],
        ),
        out_shape=[jax.ShapeDtypeStruct((TILE, pairs), jnp.int16), jax.ShapeDtypeStruct((half, cols), ints.dtype)],
        compiler_params=pltpu.CompilerParams(vmem_limit_bytes=WHOLE, dimension_semantics=("arbitrary",)),
        cost_estimate=pl.CostEstimate(flops=4_000_000, bytes_accessed=3 << 20, transcendentals=200_000),
    )(place, amps.T, amp_tiles.T, ints, tile_flags)

    swapped = lax.ppermute(away, "blk", [(b, b ^ Z) for b in range(2 * Z)])

    rings = [[h * Z + z for z in range(Z)] for h in range(2)]
    gathered = lax.all_gather(codes[None], "blk", axis=0, tiled=True, axis_index_groups=rings)
    gathered = gathered.reshape(half, pairs)

    group = STEP // (2 * ROWS)
    result = jax.ShapeDtypeStruct((2, CHIPS, ROWS, cols), jnp.float32)
    mine, theirs = pl.pallas_call(
        product_body,
        grid_spec=pltpu.PrefetchScalarGridSpec(
            num_scalar_prefetch=1,
            grid=(pairs // STEP,),
            in_specs=[
                pl.BlockSpec((half, STEP), lambda s, place: (0, s)),
                pl.BlockSpec((half, cols), lambda s, place: (place[0] // 2, 0)),
                pl.BlockSpec(tile_flags.shape, lambda s, place: (0, 0)),
                pl.BlockSpec((half, cols), lambda s, place: (0, 0)),
            ],
            out_specs=[pl.BlockSpec((2, group, ROWS, cols), lambda s, place: (0, s, 0, 0))] * 2,
            scratch_shapes=[pltpu.VMEM((half, cols), jnp.bfloat16), pltpu.VMEM((2 * Z, cols), jnp.float32)],
        ),
        out_shape=[result, result],
        compiler_params=pltpu.CompilerParams(vmem_limit_bytes=VMEM, dimension_semantics=("arbitrary",)),
        cost_estimate=pl.CostEstimate(flops=4 * pairs * half * cols, bytes_accessed=8 << 20, transcendentals=1 << 20),
    )(place, gathered, ints, tile_flags, swapped)

    theirs = lax.ppermute(theirs, "rep", [(r, r ^ 1) for r in range(2 * CHIPS)])

    peers = PEERS // Y
    block = Y * parts * ROWS + 16
    shares = pl.pallas_call(
        pack_body,
        grid=(peers,),
        in_specs=[pl.BlockSpec((1, Y, ROWS, cols), lambda s: (s // 2, s % 2, 0, 0))] * 2,
        out_specs=pl.BlockSpec((1, block, LANES), lambda s: (s, 0, 0)),
        out_shape=jax.ShapeDtypeStruct((peers, block, LANES), jnp.int16),
        compiler_params=pltpu.CompilerParams(vmem_limit_bytes=VMEM),
    )(mine, theirs)

    across = [
        [(h * Z + z) * 2 * CHIPS + g * CHIPS + 2 * y + c for h in range(2) for g in range(2)]
        for z in range(Z)
        for y in range(Y)
        for c in range(2)
    ]
    came = lax.all_to_all(shares, ("blk", "rep"), 0, 0, tiled=True, axis_index_groups=across)
    shares = pl.pallas_call(
        middle_body,
        out_shape=jax.ShapeDtypeStruct((Y, parts * ROWS + 16, LANES), jnp.int16),
        compiler_params=pltpu.CompilerParams(vmem_limit_bytes=VMEM),
    )(came)
    along = [[g * CHIPS + 2 * y + c for y in range(Y)] for g in range(2) for c in range(2)]
    shares = lax.all_to_all(shares, "rep", 0, 0, tiled=True, axis_index_groups=along)

    return pl.pallas_call(
        last_body,
        out_shape=jax.ShapeDtypeStruct((ROWS, cols), jnp.float32),
        compiler_params=pltpu.CompilerParams(vmem_limit_bytes=VMEM),
    )(shares)


def solution(mesh):
    return jax.shard_map(
        per_device,
        mesh=mesh,
        in_specs=(
            P(None, ("rep", "blk")),
            P(None, ("rep", "blk")),
            P("rep", "blk"),
            P("rep", "blk"),
        ),
        out_specs=P("rep", "blk"),
        check_vma=False,
    )
```

```python
import jax
import jax.numpy as jnp
from jax import lax
from jax.experimental import pallas as pl
from jax.experimental.pallas import tpu as pltpu
from jax.sharding import PartitionSpec as P

TILE = 64
Z = 16
CHIPS = 16
Y = 8
ROWS = 32
LANES = 128
BIAS = 253.0
STEP = 256
VMEM = 40 * 1024 * 1024
WHOLE = 62 * 1024 * 1024


def encode(amps, tiles):
    value = jnp.where(tiles > 0, amps.astype(jnp.float32), 0.0)
    size = jnp.maximum(jnp.abs(value), 2.0**-126)
    power = jnp.floor(jnp.log2(size))
    half = jnp.floor(power * 0.5)
    digits = jnp.round(size * jnp.exp2(-half) * jnp.exp2(half - power) * 128.0)
    high = digits >= 256.0
    low = digits < 128.0
    digits = jnp.where(high, digits * 0.5, jnp.where(low, digits * 2.0, digits))
    power = jnp.where(high, power + 1.0, jnp.where(low, power - 1.0, power))
    code = (power + (BIAS - 1.0)) * 128.0 + digits
    code = jnp.where(value < 0, -code, code)
    code = jnp.where(jnp.abs(value) < 2.0**-126, 0.0, code)
    return code.astype(jnp.int32).astype(jnp.int16)


def decode(codes):
    number = codes.astype(jnp.float32) * (1.0 / 128.0)
    whole = jnp.floor(jnp.abs(number))
    digits = number + jnp.where(number < 0, whole - 1.0, 1.0 - whole)
    return (digits * jnp.exp2(whole - BIAS)).astype(jnp.bfloat16)


def spread(tiles):
    shape = (tiles.shape[0], tiles.shape[0] * TILE)
    at = lax.broadcasted_iota(jnp.int32, shape, 1) // TILE == lax.broadcasted_iota(jnp.int32, shape, 0)
    return lax.dot_general(
        tiles.astype(jnp.float32), at.astype(jnp.float32), (((0,), (0,)), ((), ())), preferred_element_type=jnp.float32
    )


def keep(block, flags):
    rows = []
    for t in range(block.shape[0] // TILE):
        part = block[t * TILE : (t + 1) * TILE, :].astype(jnp.float32)
        rows.append(jnp.where(flags[t : t + 1, :] > 0, part, 0.0).astype(jnp.bfloat16))
    return jnp.concatenate(rows, axis=0)


def front_body(place, amps, tiles, ints, flags, codes, away, wide):
    step = pl.program_id(0)

    @pl.when(step == 0)
    def _():
        wide[...] = spread(flags[...])

    count = ints.shape[0] // TILE
    first = pl.multiple_of((1 - place[0] // 2 % 2) * Z + step * count, 8)
    away[...] = keep(ints[...], wide[pl.ds(first, count), :])
    codes[...] = encode(amps[...], tiles[...])


def product_body(place, codes, ints, flags, swapped, mine, mine_far, theirs, theirs_far, kept, wide):
    x_lo = place[0] // 2 % 2
    core = place[0] % 2
    half = kept.shape[0]
    wide[...] = spread(flags[...])
    own = ints[pl.ds(pl.multiple_of(x_lo * half, half), half), :]
    kept[...] = keep(own, wide[pl.ds(pl.multiple_of(x_lo * Z, Z), Z), :])
    count = STEP // (2 * ROWS)
    for s in range(codes.shape[1] // STEP):
        amps = decode(codes[:, s * STEP : (s + 1) * STEP])
        for block, ours, others in ((kept, mine, theirs), (swapped, mine_far, theirs_far)):
            total = lax.dot_general(amps, block[...], (((0,), (0,)), ((), ())), preferred_element_type=jnp.float32)
            total = total.reshape(count, 2, ROWS, total.shape[-1])
            ours[s * count : (s + 1) * count] = jnp.where(core == 0, total[:, 0], total[:, 1])
            others[s * count : (s + 1) * count] = jnp.where(core == 0, total[:, 1], total[:, 0])


def diagonal():
    shape = (ROWS, LANES)
    return lax.broadcasted_iota(jnp.int32, shape, 0) == lax.broadcasted_iota(jnp.int32, shape, 1)


def pack(totals, shares):
    lines = []
    at = 0
    for total in totals:
        top = jnp.max(jnp.abs(total), axis=1, keepdims=True)
        level = jnp.ceil(jnp.log2(jnp.maximum(top, 2.0**-110)) * 16.0)
        scaled = total * jnp.exp2(-level * (1.0 / 16.0)) * 32767.0
        whole = jnp.clip(jnp.round(scaled), -32767.0, 32767.0).astype(jnp.int32).astype(jnp.int16)
        for k in range(total.shape[1] // LANES):
            shares[at : at + ROWS, :] = whole[:, LANES * k : LANES * (k + 1)]
            at += ROWS
        lines.append(jnp.sum(jnp.where(diagonal(), level, 0.0), axis=0, keepdims=True))
    lines.append(jnp.zeros((16 - len(lines), LANES), jnp.float32))
    shares[at:, :] = jnp.concatenate(lines, axis=0).astype(jnp.int32).astype(jnp.int16)


def unpack(shares, i, parts):
    at = shares.shape[0] - 16
    line = shares[at:, :].astype(jnp.float32)[i : i + 1, :]
    level = jnp.sum(jnp.where(diagonal(), line, 0.0), axis=1, keepdims=True)
    scale = jnp.exp2(level * (1.0 / 16.0)) * (1.0 / 32767.0)
    at = i * parts * ROWS
    rows = [shares[at + ROWS * k : at + ROWS * (k + 1), :].astype(jnp.float32) * scale for k in range(parts)]
    return jnp.concatenate(rows, axis=1)


def near_body(place, mine, theirs, near):
    half = 1 - place[0] // 4
    pack([mine[half, i] + theirs[half, i] for i in range(Y)], near)


def far_body(place, mine, theirs, near, low, far):
    x_hi = place[0] // 4
    for half, shares in ((x_hi, low), (1 - x_hi, far)):
        pack([mine[half, i] + theirs[half, i] for i in range(Y)], shares)


def middle_body(place, mine, theirs, near, low, far, shares):
    parts = (shares.shape[1] - 16) // ROWS
    half = place[0] // 4
    for i in range(shares.shape[0]):
        total = mine[half, i] + theirs[half, i]
        for came in (near, low, far):
            total += unpack(came, i, parts)
        pack([total], shares.at[i])


def last_body(shares, out):
    out[...] = sum(unpack(shares.at[i], 0, out.shape[1] // LANES) for i in range(shares.shape[0]))


def per_device(amps, amp_tiles, ints, int_tiles):
    blk = lax.axis_index("blk")
    rep = lax.axis_index("rep")
    x_lo = lax.shift_right_logical(blk, 4)
    core = rep & 1
    place = (4 * lax.shift_right_logical(rep, 4) + 2 * x_lo + core).astype(jnp.int32).reshape(1)
    pairs = amps.shape[0]
    cols = ints.shape[1]
    half = ints.shape[0] // 2
    parts = cols // LANES
    tile_flags = int_tiles.T

    codes, away = pl.pallas_call(
        front_body,
        grid_spec=pltpu.PrefetchScalarGridSpec(
            num_scalar_prefetch=1,
            grid=(2,),
            in_specs=[
                pl.BlockSpec((TILE // 2, pairs), lambda s, place: (s, 0)),
                pl.BlockSpec((1, pairs), lambda s, place: (0, 0)),
                pl.BlockSpec((half // 2, cols), lambda s, place: (2 * (1 - place[0] // 2 % 2) + s, 0)),
                pl.BlockSpec(tile_flags.shape, lambda s, place: (0, 0)),
            ],
            out_specs=[
                pl.BlockSpec((TILE // 2, pairs), lambda s, place: (s, 0)),
                pl.BlockSpec((half // 2, cols), lambda s, place: (s, 0)),
            ],
            scratch_shapes=[pltpu.VMEM((2 * Z, cols), jnp.float32)],
        ),
        out_shape=[jax.ShapeDtypeStruct((TILE, pairs), jnp.int16), jax.ShapeDtypeStruct((half, cols), ints.dtype)],
        compiler_params=pltpu.CompilerParams(vmem_limit_bytes=WHOLE, dimension_semantics=("arbitrary",)),
        cost_estimate=pl.CostEstimate(flops=4_000_000, bytes_accessed=3 << 20, transcendentals=200_000),
    )(place, amps.T, amp_tiles.T, ints, tile_flags)

    swapped = lax.ppermute(away, "blk", [(b, b ^ Z) for b in range(2 * Z)])

    rings = [[h * Z + z for z in range(Z)] for h in range(2)]
    gathered = lax.all_gather(codes[None], "blk", axis=0, tiled=True, axis_index_groups=rings)
    gathered = gathered.reshape(half, pairs)

    inside = pl.BlockSpec(memory_space=pltpu.VMEM)
    scalar = pl.BlockSpec(memory_space=pltpu.SMEM)
    result = jax.ShapeDtypeStruct((CHIPS, ROWS, cols), jnp.float32)
    mine, mine_far, theirs, theirs_far = pl.pallas_call(
        product_body,
        in_specs=[scalar] + [inside] * 4,
        out_specs=[inside] * 4,
        scratch_shapes=[pltpu.VMEM((half, cols), jnp.bfloat16), pltpu.VMEM((2 * Z, cols), jnp.float32)],
        out_shape=[result] * 4,
        compiler_params=pltpu.CompilerParams(vmem_limit_bytes=VMEM),
        cost_estimate=pl.CostEstimate(flops=4 * pairs * half * cols, bytes_accessed=8 << 20, transcendentals=1 << 20),
    )(place, gathered, ints, tile_flags, swapped)

    n = 2 * CHIPS
    swap = [(r, r ^ 1) for r in range(n)]
    theirs = lax.ppermute(theirs, "rep", swap).reshape(2, Y, ROWS, cols)
    theirs_far = lax.ppermute(theirs_far, "rep", swap).reshape(2, Y, ROWS, cols)
    mine = mine.reshape(2, Y, ROWS, cols)
    mine_far = mine_far.reshape(2, Y, ROWS, cols)

    block = Y * parts * ROWS + 16
    sent = jax.ShapeDtypeStruct((block, LANES), jnp.int16)
    near = pl.pallas_call(
        near_body,
        in_specs=[scalar, inside, inside],
        out_specs=inside,
        out_shape=sent,
        compiler_params=pltpu.CompilerParams(vmem_limit_bytes=VMEM),
        cost_estimate=pl.CostEstimate(flops=4 << 20, bytes_accessed=2 << 20, transcendentals=0),
    )(place, mine, theirs)
    low, far = pl.pallas_call(
        far_body,
        in_specs=[scalar, inside, inside, pl.BlockSpec(memory_space=pl.ANY)],
        out_specs=[inside, inside],
        out_shape=[sent, sent],
        compiler_params=pltpu.CompilerParams(vmem_limit_bytes=VMEM),
        cost_estimate=pl.CostEstimate(flops=8 << 20, bytes_accessed=4 << 20, transcendentals=0),
    )(place, mine_far, theirs_far, near)
    near = lax.ppermute(near, "rep", [(r, r ^ CHIPS) for r in range(n)])
    low = lax.ppermute(low, "blk", [(b, b ^ Z) for b in range(2 * Z)])
    far = lax.ppermute(
        far, ("blk", "rep"), [(b * n + r, (b ^ Z) * n + (r ^ CHIPS)) for b in range(2 * Z) for r in range(n)]
    )
    shares = pl.pallas_call(
        middle_body,
        in_specs=[scalar] + [inside] * 5,
        out_specs=inside,
        out_shape=jax.ShapeDtypeStruct((Y, parts * ROWS + 16, LANES), jnp.int16),
        compiler_params=pltpu.CompilerParams(vmem_limit_bytes=VMEM),
    )(place, mine, theirs, near, low, far)
    along = [[g * CHIPS + 2 * y + c for y in range(Y)] for g in range(2) for c in range(2)]
    shares = lax.all_to_all(shares, "rep", 0, 0, tiled=True, axis_index_groups=along)

    return pl.pallas_call(
        last_body,
        out_shape=jax.ShapeDtypeStruct((ROWS, cols), jnp.float32),
        compiler_params=pltpu.CompilerParams(vmem_limit_bytes=VMEM),
    )(shares)


def solution(mesh):
    return jax.shard_map(
        per_device,
        mesh=mesh,
        in_specs=(
            P(None, ("rep", "blk")),
            P(None, ("rep", "blk")),
            P("rep", "blk"),
            P("rep", "blk"),
        ),
        out_specs=P("rep", "blk"),
        check_vma=False,
    )
```

```python
import jax
import jax.numpy as jnp
from jax import lax
from jax.experimental import pallas as pl
from jax.experimental.pallas import tpu as pltpu
from jax.sharding import PartitionSpec as P

TILE = 64
Z = 16
CHIPS = 16
Y = 8
ROWS = 32
LANES = 128
BIAS = 253.0
STEP = 256
VMEM = 40 * 1024 * 1024
WHOLE = 62 * 1024 * 1024


def encode(amps, tiles):
    value = jnp.where(tiles > 0, amps.astype(jnp.float32), 0.0)
    size = jnp.maximum(jnp.abs(value), 2.0**-126)
    power = jnp.floor(jnp.log2(size))
    half = jnp.floor(power * 0.5)
    digits = jnp.round(size * jnp.exp2(-half) * jnp.exp2(half - power) * 128.0)
    high = digits >= 256.0
    low = digits < 128.0
    digits = jnp.where(high, digits * 0.5, jnp.where(low, digits * 2.0, digits))
    power = jnp.where(high, power + 1.0, jnp.where(low, power - 1.0, power))
    code = (power + (BIAS - 1.0)) * 128.0 + digits
    code = jnp.where(value < 0, -code, code)
    code = jnp.where(jnp.abs(value) < 2.0**-126, 0.0, code)
    return code.astype(jnp.int32).astype(jnp.int16)


def decode(codes):
    number = codes.astype(jnp.float32) * (1.0 / 128.0)
    whole = jnp.floor(jnp.abs(number))
    digits = number + jnp.where(number < 0, whole - 1.0, 1.0 - whole)
    return (digits * jnp.exp2(whole - BIAS)).astype(jnp.bfloat16)


def spread(tiles):
    shape = (tiles.shape[0], tiles.shape[0] * TILE)
    at = lax.broadcasted_iota(jnp.int32, shape, 1) // TILE == lax.broadcasted_iota(jnp.int32, shape, 0)
    return lax.dot_general(
        tiles.astype(jnp.float32), at.astype(jnp.float32), (((0,), (0,)), ((), ())), preferred_element_type=jnp.float32
    )


def keep(block, flags):
    rows = []
    for t in range(block.shape[0] // TILE):
        part = block[t * TILE : (t + 1) * TILE, :].astype(jnp.float32)
        rows.append(jnp.where(flags[t : t + 1, :] > 0, part, 0.0).astype(jnp.bfloat16))
    return jnp.concatenate(rows[::-1], axis=0)


def front_body(place, amps, tiles, ints, flags, codes, away, wide):
    step = pl.program_id(0)

    @pl.when(step == 0)
    def _():
        wide[...] = spread(flags[...])

    count = ints.shape[0] // TILE
    first = pl.multiple_of((1 - place[0] // 2 % 2) * Z + step * count, 8)
    away[...] = keep(ints[...], wide[pl.ds(first, count), :])
    codes[...] = encode(amps[...], tiles[...])


def product_body(place, codes, ints, flags, swapped, mine, mine_far, theirs, theirs_far, kept, wide):
    x_lo = place[0] // 2 % 2
    core = place[0] % 2
    half = kept.shape[0]
    wide[...] = spread(flags[...])
    own = ints[pl.ds(pl.multiple_of(x_lo * half, half), half), :]
    kept[...] = keep(own, wide[pl.ds(pl.multiple_of(x_lo * Z, Z), Z), :])
    count = STEP // (2 * ROWS)
    for s in range(codes.shape[1] // STEP):
        amps = decode(codes[:, s * STEP : (s + 1) * STEP])
        for block, ours, others in ((kept, mine, theirs), (swapped, mine_far, theirs_far)):
            total = lax.dot_general(amps, block[...], (((0,), (0,)), ((), ())), preferred_element_type=jnp.float32)
            total = total.reshape(count, 2, ROWS, total.shape[-1])
            ours[s * count : (s + 1) * count] = jnp.where(core == 0, total[:, 0], total[:, 1])
            others[s * count : (s + 1) * count] = jnp.where(core == 0, total[:, 1], total[:, 0])


def diagonal():
    shape = (ROWS, LANES)
    return lax.broadcasted_iota(jnp.int32, shape, 0) == lax.broadcasted_iota(jnp.int32, shape, 1)


def pack(totals, shares):
    lines = []
    at = 0
    for total in totals:
        top = jnp.max(jnp.abs(total), axis=1, keepdims=True)
        level = jnp.ceil(jnp.log2(jnp.maximum(top, 2.0**-110)) * 16.0)
        scaled = total * jnp.exp2(-level * (1.0 / 16.0)) * 32767.0
        whole = jnp.clip(jnp.round(scaled), -32767.0, 32767.0).astype(jnp.int32).astype(jnp.int16)
        for k in range(total.shape[1] // LANES):
            shares[at : at + ROWS, :] = whole[:, LANES * k : LANES * (k + 1)]
            at += ROWS
        lines.append(jnp.sum(jnp.where(diagonal(), level, 0.0), axis=0, keepdims=True))
    lines.append(jnp.zeros((16 - len(lines), LANES), jnp.float32))
    shares[at:, :] = jnp.concatenate(lines, axis=0).astype(jnp.int32).astype(jnp.int16)


def unpack(shares, i, parts):
    at = shares.shape[0] - 16
    line = shares[at:, :].astype(jnp.float32)[i : i + 1, :]
    level = jnp.sum(jnp.where(diagonal(), line, 0.0), axis=1, keepdims=True)
    scale = jnp.exp2(level * (1.0 / 16.0)) * (1.0 / 32767.0)
    at = i * parts * ROWS
    rows = [shares[at + ROWS * k : at + ROWS * (k + 1), :].astype(jnp.float32) * scale for k in range(parts)]
    return jnp.concatenate(rows, axis=1)


def near_body(place, mine, theirs, near):
    half = 1 - place[0] // 4
    pack([mine[half, i] + theirs[half, i] for i in range(Y)], near)


def far_body(place, mine, theirs, near, low, far):
    x_hi = place[0] // 4
    for half, shares in ((x_hi, low), (1 - x_hi, far)):
        pack([mine[half, i] + theirs[half, i] for i in range(Y)], shares)


def middle_body(place, mine, theirs, near, low, far, shares):
    parts = (shares.shape[1] - 16) // ROWS
    half = place[0] // 4
    for i in range(shares.shape[0]):
        total = mine[half, i] + theirs[half, i]
        for came in (near, low, far):
            total += unpack(came, i, parts)
        pack([total], shares.at[i])


def last_body(shares, out):
    out[...] = sum(unpack(shares.at[i], 0, out.shape[1] // LANES) for i in range(shares.shape[0]))


def per_device(amps, amp_tiles, ints, int_tiles):
    blk = lax.axis_index("blk")
    rep = lax.axis_index("rep")
    x_lo = lax.shift_right_logical(blk, 4)
    core = rep & 1
    place = (4 * lax.shift_right_logical(rep, 4) + 2 * x_lo + core).astype(jnp.int32).reshape(1)
    pairs = amps.shape[0]
    cols = ints.shape[1]
    half = ints.shape[0] // 2
    parts = cols // LANES
    tile_flags = int_tiles.T

    codes, away = pl.pallas_call(
        front_body,
        grid_spec=pltpu.PrefetchScalarGridSpec(
            num_scalar_prefetch=1,
            grid=(2,),
            in_specs=[
                pl.BlockSpec((TILE // 2, pairs), lambda s, place: (s, 0)),
                pl.BlockSpec((1, pairs), lambda s, place: (0, 0)),
                pl.BlockSpec((half // 2, cols), lambda s, place: (2 * (1 - place[0] // 2 % 2) + s, 0)),
                pl.BlockSpec(tile_flags.shape, lambda s, place: (0, 0)),
            ],
            out_specs=[
                pl.BlockSpec((TILE // 2, pairs), lambda s, place: (s, 0)),
                pl.BlockSpec((half // 2, cols), lambda s, place: (1 - s, 0)),
            ],
            scratch_shapes=[pltpu.VMEM((2 * Z, cols), jnp.float32)],
        ),
        out_shape=[jax.ShapeDtypeStruct((TILE, pairs), jnp.int16), jax.ShapeDtypeStruct((half, cols), ints.dtype)],
        compiler_params=pltpu.CompilerParams(vmem_limit_bytes=WHOLE, dimension_semantics=("arbitrary",)),
        cost_estimate=pl.CostEstimate(flops=4_000_000, bytes_accessed=3 << 20, transcendentals=200_000),
    )(place, amps.T, amp_tiles.T, ints, tile_flags)

    swapped = lax.ppermute(away, "blk", [(b, b ^ Z) for b in range(2 * Z)])

    rings = [[h * Z + z for z in reversed(range(Z))] for h in range(2)]
    gathered = lax.all_gather(codes[None], "blk", axis=0, tiled=True, axis_index_groups=rings)
    gathered = gathered.reshape(half, pairs)

    inside = pl.BlockSpec(memory_space=pltpu.VMEM)
    scalar = pl.BlockSpec(memory_space=pltpu.SMEM)
    result = jax.ShapeDtypeStruct((CHIPS, ROWS, cols), jnp.float32)
    mine, mine_far, theirs, theirs_far = pl.pallas_call(
        product_body,
        in_specs=[scalar] + [inside] * 4,
        out_specs=[inside] * 4,
        scratch_shapes=[pltpu.VMEM((half, cols), jnp.bfloat16), pltpu.VMEM((2 * Z, cols), jnp.float32)],
        out_shape=[result] * 4,
        compiler_params=pltpu.CompilerParams(vmem_limit_bytes=VMEM),
        cost_estimate=pl.CostEstimate(flops=4 * pairs * half * cols, bytes_accessed=8 << 20, transcendentals=1 << 20),
    )(place, gathered, ints, tile_flags, swapped)

    n = 2 * CHIPS
    swap = [(r, r ^ 1) for r in range(n)]
    theirs = lax.ppermute(theirs, "rep", swap).reshape(2, Y, ROWS, cols)
    theirs_far = lax.ppermute(theirs_far, "rep", swap).reshape(2, Y, ROWS, cols)
    mine = mine.reshape(2, Y, ROWS, cols)
    mine_far = mine_far.reshape(2, Y, ROWS, cols)

    block = Y * parts * ROWS + 16
    sent = jax.ShapeDtypeStruct((block, LANES), jnp.int16)
    near = pl.pallas_call(
        near_body,
        in_specs=[scalar, inside, inside],
        out_specs=inside,
        out_shape=sent,
        compiler_params=pltpu.CompilerParams(vmem_limit_bytes=VMEM),
        cost_estimate=pl.CostEstimate(flops=4 << 20, bytes_accessed=2 << 20, transcendentals=0),
    )(place, mine, theirs)
    low, far = pl.pallas_call(
        far_body,
        in_specs=[scalar, inside, inside, pl.BlockSpec(memory_space=pl.ANY)],
        out_specs=[inside, inside],
        out_shape=[sent, sent],
        compiler_params=pltpu.CompilerParams(vmem_limit_bytes=VMEM),
        cost_estimate=pl.CostEstimate(flops=8 << 20, bytes_accessed=4 << 20, transcendentals=0),
    )(place, mine_far, theirs_far, near)
    near = lax.ppermute(near, "rep", [(r, r ^ CHIPS) for r in range(n)])
    low = lax.ppermute(low, "blk", [(b, b ^ Z) for b in range(2 * Z)])
    far = lax.ppermute(
        far, ("blk", "rep"), [(b * n + r, (b ^ Z) * n + (r ^ CHIPS)) for b in range(2 * Z) for r in range(n)]
    )
    shares = pl.pallas_call(
        middle_body,
        in_specs=[scalar] + [inside] * 5,
        out_specs=inside,
        out_shape=jax.ShapeDtypeStruct((Y, parts * ROWS + 16, LANES), jnp.int16),
        compiler_params=pltpu.CompilerParams(vmem_limit_bytes=VMEM),
    )(place, mine, theirs, near, low, far)
    along = [[g * CHIPS + 2 * y + c for y in range(Y)] for g in range(2) for c in range(2)]
    shares = lax.all_to_all(shares, "rep", 0, 0, tiled=True, axis_index_groups=along)

    return pl.pallas_call(
        last_body,
        out_shape=jax.ShapeDtypeStruct((ROWS, cols), jnp.float32),
        compiler_params=pltpu.CompilerParams(vmem_limit_bytes=VMEM),
    )(shares)


def solution(mesh):
    return jax.shard_map(
        per_device,
        mesh=mesh,
        in_specs=(
            P(None, ("rep", "blk")),
            P(None, ("rep", "blk")),
            P("rep", "blk"),
            P("rep", "blk"),
        ),
        out_specs=P("rep", "blk"),
        check_vma=False,
    )
```

```python
import jax
import jax.numpy as jnp
from jax import lax
from jax.experimental import pallas as pl
from jax.experimental.pallas import tpu as pltpu
from jax.sharding import PartitionSpec as P

TILE = 64
Z = 16
CHIPS = 16
Y = 8
ROWS = 32
LANES = 128
BIAS = 253.0
STEP = 256
VMEM = 40 * 1024 * 1024
WHOLE = 62 * 1024 * 1024


def encode(amps, tiles):
    value = jnp.where(tiles > 0, amps.astype(jnp.float32), 0.0)
    size = jnp.maximum(jnp.abs(value), 2.0**-126)
    power = jnp.floor(jnp.log2(size))
    half = jnp.floor(power * 0.5)
    digits = jnp.round(size * jnp.exp2(-half) * jnp.exp2(half - power) * 128.0)
    high = digits >= 256.0
    low = digits < 128.0
    digits = jnp.where(high, digits * 0.5, jnp.where(low, digits * 2.0, digits))
    power = jnp.where(high, power + 1.0, jnp.where(low, power - 1.0, power))
    code = (power + (BIAS - 1.0)) * 128.0 + digits
    code = jnp.where(value < 0, -code, code)
    code = jnp.where(jnp.abs(value) < 2.0**-126, 0.0, code)
    return code.astype(jnp.int32).astype(jnp.int16)


def decode(codes):
    number = codes.astype(jnp.float32) * (1.0 / 128.0)
    whole = jnp.floor(jnp.abs(number))
    digits = number + jnp.where(number < 0, whole - 1.0, 1.0 - whole)
    return (digits * jnp.exp2(whole - BIAS)).astype(jnp.bfloat16)


def spread(tiles):
    shape = (tiles.shape[0], tiles.shape[0] * TILE)
    at = lax.broadcasted_iota(jnp.int32, shape, 1) // TILE == lax.broadcasted_iota(jnp.int32, shape, 0)
    return lax.dot_general(
        tiles.astype(jnp.float32), at.astype(jnp.float32), (((0,), (0,)), ((), ())), preferred_element_type=jnp.float32
    )


def keep(block, flags):
    rows = []
    for t in range(block.shape[0] // TILE):
        part = block[t * TILE : (t + 1) * TILE, :].astype(jnp.float32)
        rows.append(jnp.where(flags[t : t + 1, :] > 0, part, 0.0).astype(jnp.bfloat16))
    return jnp.concatenate(rows[::-1], axis=0)


def front_body(place, amps, tiles, ints, flags, codes, away, wide):
    step = pl.program_id(0)

    @pl.when(step == 0)
    def _():
        wide[...] = spread(flags[...])

    count = ints.shape[0] // TILE
    first = pl.multiple_of((1 - place[0] // 2 % 2) * Z + step * count, 8)
    away[...] = keep(ints[...], wide[pl.ds(first, count), :])
    codes[...] = encode(amps[...], tiles[...])


def product_body(place, codes, ints, flags, swapped, mine, mine_far, theirs, theirs_far, kept, wide):
    x_lo = place[0] // 2 % 2
    core = place[0] % 2
    half = kept.shape[0]
    wide[...] = spread(flags[...])
    own = ints[pl.ds(pl.multiple_of(x_lo * half, half), half), :]
    kept[...] = keep(own, wide[pl.ds(pl.multiple_of(x_lo * Z, Z), Z), :])
    count = STEP // (2 * ROWS)
    for s in range(codes.shape[1] // STEP):
        amps = decode(codes[:, s * STEP : (s + 1) * STEP])
        for block, ours, others in ((kept, mine, theirs), (swapped, mine_far, theirs_far)):
            total = lax.dot_general(amps, block[...], (((0,), (0,)), ((), ())), preferred_element_type=jnp.float32)
            total = total.reshape(count, 2, ROWS, total.shape[-1])
            ours[s * count : (s + 1) * count] = jnp.where(core == 0, total[:, 0], total[:, 1])
            others[s * count : (s + 1) * count] = jnp.where(core == 0, total[:, 1], total[:, 0])


def diagonal():
    shape = (ROWS, LANES)
    return lax.broadcasted_iota(jnp.int32, shape, 0) == lax.broadcasted_iota(jnp.int32, shape, 1)


def pack(totals, shares):
    lines = []
    at = 0
    for total in totals:
        top = jnp.max(jnp.abs(total), axis=1, keepdims=True)
        level = jnp.ceil(jnp.log2(jnp.maximum(top, 2.0**-110)) * 16.0)
        scaled = total * jnp.exp2(-level * (1.0 / 16.0)) * 32767.0
        whole = jnp.clip(jnp.round(scaled), -32767.0, 32767.0).astype(jnp.int32).astype(jnp.int16)
        for k in range(total.shape[1] // LANES):
            shares[at : at + ROWS, :] = whole[:, LANES * k : LANES * (k + 1)]
            at += ROWS
        lines.append(jnp.sum(jnp.where(diagonal(), level, 0.0), axis=0, keepdims=True))
    lines.append(jnp.zeros((16 - len(lines), LANES), jnp.float32))
    shares[at:, :] = jnp.concatenate(lines, axis=0).astype(jnp.int32).astype(jnp.int16)


def unpack(shares, i, parts):
    at = shares.shape[0] - 16
    line = shares[at:, :].astype(jnp.float32)[i : i + 1, :]
    level = jnp.sum(jnp.where(diagonal(), line, 0.0), axis=1, keepdims=True)
    scale = jnp.exp2(level * (1.0 / 16.0)) * (1.0 / 32767.0)
    at = i * parts * ROWS
    rows = [shares[at + ROWS * k : at + ROWS * (k + 1), :].astype(jnp.float32) * scale for k in range(parts)]
    return jnp.concatenate(rows, axis=1)


def near_body(place, mine, theirs, near):
    half = 1 - place[0] // 4
    pack([mine[half, i] + theirs[half, i] for i in range(Y)], near)


def far_body(place, mine, theirs, near, low, far):
    x_hi = place[0] // 4
    for half, shares in ((x_hi, low), (1 - x_hi, far)):
        pack([mine[half, i] + theirs[half, i] for i in range(Y)], shares)


def middle_body(place, mine, theirs, near, low, far, shares):
    parts = (shares.shape[1] - 16) // ROWS
    half = place[0] // 4
    for i in range(shares.shape[0]):
        total = mine[half, i] + theirs[half, i]
        for came in (near, low, far):
            total += unpack(came, i, parts)
        pack([total], shares.at[Y - 1 - i])


def last_body(shares, out):
    out[...] = sum(unpack(shares.at[i], 0, out.shape[1] // LANES) for i in range(shares.shape[0]))


def per_device(amps, amp_tiles, ints, int_tiles):
    blk = lax.axis_index("blk")
    rep = lax.axis_index("rep")
    x_lo = lax.shift_right_logical(blk, 4)
    core = rep & 1
    place = (4 * lax.shift_right_logical(rep, 4) + 2 * x_lo + core).astype(jnp.int32).reshape(1)
    pairs = amps.shape[0]
    cols = ints.shape[1]
    half = ints.shape[0] // 2
    parts = cols // LANES
    tile_flags = int_tiles.T

    codes, away = pl.pallas_call(
        front_body,
        grid_spec=pltpu.PrefetchScalarGridSpec(
            num_scalar_prefetch=1,
            grid=(2,),
            in_specs=[
                pl.BlockSpec((TILE // 2, pairs), lambda s, place: (s, 0)),
                pl.BlockSpec((1, pairs), lambda s, place: (0, 0)),
                pl.BlockSpec((half // 2, cols), lambda s, place: (2 * (1 - place[0] // 2 % 2) + s, 0)),
                pl.BlockSpec(tile_flags.shape, lambda s, place: (0, 0)),
            ],
            out_specs=[
                pl.BlockSpec((TILE // 2, pairs), lambda s, place: (s, 0)),
                pl.BlockSpec((half // 2, cols), lambda s, place: (1 - s, 0)),
            ],
            scratch_shapes=[pltpu.VMEM((2 * Z, cols), jnp.float32)],
        ),
        out_shape=[jax.ShapeDtypeStruct((TILE, pairs), jnp.int16), jax.ShapeDtypeStruct((half, cols), ints.dtype)],
        compiler_params=pltpu.CompilerParams(vmem_limit_bytes=WHOLE, dimension_semantics=("arbitrary",)),
        cost_estimate=pl.CostEstimate(flops=4_000_000, bytes_accessed=3 << 20, transcendentals=200_000),
    )(place, amps.T, amp_tiles.T, ints, tile_flags)

    swapped = lax.ppermute(away, "blk", [(b, b ^ Z) for b in range(2 * Z)])

    rings = [[h * Z + z for z in reversed(range(Z))] for h in range(2)]
    gathered = lax.all_gather(codes[None], "blk", axis=0, tiled=True, axis_index_groups=rings)
    gathered = gathered.reshape(half, pairs)

    inside = pl.BlockSpec(memory_space=pltpu.VMEM)
    scalar = pl.BlockSpec(memory_space=pltpu.SMEM)
    result = jax.ShapeDtypeStruct((CHIPS, ROWS, cols), jnp.float32)
    mine, mine_far, theirs, theirs_far = pl.pallas_call(
        product_body,
        in_specs=[scalar] + [inside] * 4,
        out_specs=[inside] * 4,
        scratch_shapes=[pltpu.VMEM((half, cols), jnp.bfloat16), pltpu.VMEM((2 * Z, cols), jnp.float32)],
        out_shape=[result] * 4,
        compiler_params=pltpu.CompilerParams(vmem_limit_bytes=VMEM),
        cost_estimate=pl.CostEstimate(flops=4 * pairs * half * cols, bytes_accessed=8 << 20, transcendentals=1 << 20),
    )(place, gathered, ints, tile_flags, swapped)

    n = 2 * CHIPS
    swap = [(r, r ^ 1) for r in range(n)]
    theirs = lax.ppermute(theirs, "rep", swap).reshape(2, Y, ROWS, cols)
    theirs_far = lax.ppermute(theirs_far, "rep", swap).reshape(2, Y, ROWS, cols)
    mine = mine.reshape(2, Y, ROWS, cols)
    mine_far = mine_far.reshape(2, Y, ROWS, cols)

    block = Y * parts * ROWS + 16
    sent = jax.ShapeDtypeStruct((block, LANES), jnp.int16)
    near = pl.pallas_call(
        near_body,
        in_specs=[scalar, inside, inside],
        out_specs=inside,
        out_shape=sent,
        compiler_params=pltpu.CompilerParams(vmem_limit_bytes=VMEM),
        cost_estimate=pl.CostEstimate(flops=4 << 20, bytes_accessed=2 << 20, transcendentals=0),
    )(place, mine, theirs)
    low, far = pl.pallas_call(
        far_body,
        in_specs=[scalar, inside, inside, pl.BlockSpec(memory_space=pl.ANY)],
        out_specs=[inside, inside],
        out_shape=[sent, sent],
        compiler_params=pltpu.CompilerParams(vmem_limit_bytes=VMEM),
        cost_estimate=pl.CostEstimate(flops=8 << 20, bytes_accessed=4 << 20, transcendentals=0),
    )(place, mine_far, theirs_far, near)
    near = lax.ppermute(near, "rep", [(r, r ^ CHIPS) for r in range(n)])
    low = lax.ppermute(low, "blk", [(b, b ^ Z) for b in range(2 * Z)])
    far = lax.ppermute(
        far, ("blk", "rep"), [(b * n + r, (b ^ Z) * n + (r ^ CHIPS)) for b in range(2 * Z) for r in range(n)]
    )
    shares = pl.pallas_call(
        middle_body,
        in_specs=[scalar] + [inside] * 5,
        out_specs=inside,
        out_shape=jax.ShapeDtypeStruct((Y, parts * ROWS + 16, LANES), jnp.int16),
        compiler_params=pltpu.CompilerParams(vmem_limit_bytes=VMEM),
    )(place, mine, theirs, near, low, far)
    along = [[g * CHIPS + 2 * y + c for y in reversed(range(Y))] for g in range(2) for c in range(2)]
    shares = lax.all_to_all(shares, "rep", 0, 0, tiled=True, axis_index_groups=along)

    return pl.pallas_call(
        last_body,
        out_shape=jax.ShapeDtypeStruct((ROWS, cols), jnp.float32),
        compiler_params=pltpu.CompilerParams(vmem_limit_bytes=VMEM),
    )(shares)


def solution(mesh):
    return jax.shard_map(
        per_device,
        mesh=mesh,
        in_specs=(
            P(None, ("rep", "blk")),
            P(None, ("rep", "blk")),
            P("rep", "blk"),
            P("rep", "blk"),
        ),
        out_specs=P("rep", "blk"),
        check_vma=False,
    )
```
